32 devices in a mesh: seq: 8 (over z, y), head: 4 (over x, core).
Axes of the slice: x: 2, y: 2, z: 4, core: 2. Of those that a mesh axis runs over, the one named last changes fastest.
Arguments:
- byte_states: bfloat16 [6144, 1280], P('seq', 'head'), may hold values from -19 to 19
- patch_ids: int32 [6144], P('seq'), may hold values from 0 to 767, never falling along the last dimension, each value on 1 to 16 neighbouring positions
- slot_patch: int32 [768], replicated, may hold values from 0 to 767, each once
- pool_gain: float32 [1280], replicated, may hold values from 0.25 to 1.75
- w_in: bfloat16 [1280, 4096], P('seq', 'head'), may hold values from -0.16910264 to 0.16910264
- attn_gain: float32 [4096], replicated, may hold values from 0.25 to 1.75
- w_qkv: bfloat16 [4096, 3, 1024], P('seq', None, 'head'), may hold values from -0.5105401 to 0.5105401
- w_out: bfloat16 [1024, 4096], P('head'), may hold values from -0.1875 to 0.1875
- w_down: bfloat16 [4096, 1280], P('head', 'seq'), may hold values from -0.34375 to 0.34375
Outputs:
- patch_out: bfloat16 [768, 4096], P('seq', 'head')
- byte_out: bfloat16 [6144, 1280], P('seq', 'head')
The draws below stay inside these ranges and needn't reach their ends.
Inputs may be any that keep to these rules, and one draw needn't show every extreme that they name: patch_ids never falls along the bytes; each of the 768 patches holds 1 to 16 consecutive bytes, and some patch exactly 16. `slot_patch`: every patch number appears once; slot r belongs to segment r // 96.
All inputs are finite; a program needn't handle non-finite values.
Results may differ from the reference program's by a relative error of at most 0.015.
Values may be sent and summed in bfloat16 or wider, within the bound.
A program may use at most 64 MiB of HBM per device.

```python
import math
from functools import partial
import jax
import jax.numpy as jnp
import numpy as np
from jax import lax

BYTE_WIDTH = 1280
MODEL_WIDTH = 4096
HEAD_SIZE = 128
LONGEST = 16
WINDOW = 8
BYTES_DEV = 768
BYTES = 6144
PATCHES = 768
HEADS = 8
N_SEQ = 8
N_HEAD = 4


def input_matrix(key):
    return jax.random.truncated_normal(jax.random.fold_in(key, 7101), -6.0, 6.0, (BYTE_WIDTH, MODEL_WIDTH), jnp.float32) / math.sqrt(BYTE_WIDTH)


def draw_w_in(key, part):
    return input_matrix(key).astype(jnp.bfloat16)


def draw_w_down(key, part):
    spread_part = jax.random.truncated_normal(jax.random.fold_in(key, 7102), -6.0, 6.0, (MODEL_WIDTH, BYTE_WIDTH), jnp.float32) / math.sqrt(MODEL_WIDTH)
    return spread_part.astype(jnp.bfloat16)


def draw_w_qkv(key, part):
    normal_part = jax.random.truncated_normal(jax.random.fold_in(key, 7201), -6.0, 6.0, (MODEL_WIDTH, 3, HEADS * HEAD_SIZE), jnp.float32) / math.sqrt(MODEL_WIDTH)
    ranking = jax.random.permutation(jax.random.fold_in(key, 7202), HEADS)
    strong_count = max(1, HEADS // 4)
    levels = jnp.clip(strong_count - 1 - ranking, 0, strong_count - 1).astype(jnp.float32)
    strength = 330.0 * (1.0 / 3.0) ** (levels / max(strong_count - 1, 1))
    factor = jnp.repeat(jnp.sqrt(strength / math.sqrt(HEAD_SIZE)), HEAD_SIZE)
    strong = jnp.repeat(ranking < strong_count, HEAD_SIZE)
    queries = normal_part[:, 0, :]
    aligned = factor[None, :] * queries
    query_part = jnp.where(strong[None, :], aligned, queries)
    key_part = jnp.where(strong[None, :], aligned, normal_part[:, 1, :])
    return jnp.stack([query_part, key_part, normal_part[:, 2, :]], axis=1).astype(jnp.bfloat16)


def slow_field(key):
    coeffs = jax.random.normal(jax.random.fold_in(key, 7304), (3,), jnp.float32)
    phases = jax.random.uniform(jax.random.fold_in(key, 7305), (3,), jnp.float32, 0.0, 2.0 * math.pi)
    position = jnp.arange(BYTES, dtype=jnp.float32) / BYTES
    rates = jnp.arange(1, 4, dtype=jnp.float32)
    field = jnp.sum(coeffs[:, None] * jnp.sin(2.0 * math.pi * rates[:, None] * position[None, :] + phases[:, None]), axis=0)
    return field / (jnp.max(jnp.abs(field)) + 1e-06)


def draw_byte_states(key, part):
    rough_part = jax.random.truncated_normal(jax.random.fold_in(key, 7301), -6.0, 6.0, (BYTES, BYTE_WIDTH), jnp.float32)
    common = jax.random.truncated_normal(jax.random.fold_in(key, 7302), -2.5, 2.5, (BYTE_WIDTH,), jnp.float32)
    field = slow_field(key)
    return (2.0 * field[:, None] * common[None, :] + rough_part).astype(jnp.bfloat16)


def level_of(rng, dims, cuts, smallest, top_value):
    level = 1.0
    for dim, shards_of in cuts:
        draws = jax.random.uniform(jax.random.fold_in(jax.random.fold_in(rng, 6), dim), (shards_of,), jnp.float32, smallest / len(cuts), top_value / len(cuts))
        level = level * jnp.repeat(jnp.exp(draws), dims[dim] // shards_of).reshape((-1,) + (1,) * (len(dims) - 1 - dim))
    return level


def split_up(number_of, total, most, lean):
    weights = [(1 << 20) // math.isqrt(grade ** lean) + 1 for grade in range(2, number_of + 1)]
    spare, counts = total - most - (number_of - 1), [1] * (number_of - 1)
    while spare > 0:
        candidates = [i for i in range(number_of - 1) if counts[i] < most]
        whole, left = sum([weights[i] for i in candidates]), spare
        for i in candidates:
            extra = min(most - counts[i], max(1, left * weights[i] // whole), spare)
            counts[i] = counts[i] + extra
            spare = spare - extra
    return np.array([most] + counts)


def uneven(key, amount, total, bound, skew):
    if amount == 2:
        one = jax.random.randint(key, (), max(1, total - bound), min(bound, total - 1) + 1)
        return jnp.stack([one, total - one])
    sizes = jnp.asarray(split_up(amount, total, bound, skew), jnp.int32)
    couples = (amount - 1) // 2
    source_of, receiver = sizes[1:1 + 2 * couples:2], sizes[2:2 + 2 * couples:2]
    margin = jnp.minimum(source_of - 1, bound - receiver)
    passed = jax.random.randint(jax.random.fold_in(key, 1), (couples,), 0, 1 << 20) % (margin + 1)
    sizes = sizes.at[1:1 + 2 * couples:2].set(source_of - passed).at[2:2 + 2 * couples:2].set(receiver + passed)
    return sizes[jax.random.permutation(jax.random.fold_in(key, 2), amount)]


def normal_values(own_key, shape, scale, most, cuts=(), kind=jnp.bfloat16):
    values = jax.random.normal(own_key, shape, jnp.float32) * scale
    if len(cuts) > 0:
        values = level_of(own_key, shape, cuts, -0.22, 0.18) * values
    return jnp.clip(values, min=-most, max=most).astype(kind)


def setup_inputs(seed: int = 0) -> dict:
    key_list = jax.random.split(jax.random.key(seed), 10)
    return {
        "byte_states": draw_byte_states(jax.random.fold_in(key_list[9], 71), 0),
        "patch_ids": jnp.searchsorted(jnp.cumsum(uneven(key_list[1], PATCHES, BYTES, LONGEST, 2)), jnp.arange(BYTES), side="right").astype(jnp.int32),
        "slot_patch": jax.random.permutation(key_list[2], PATCHES).astype(jnp.int32),
        "pool_gain": jnp.clip(1.0 + 0.15 * jax.random.normal(key_list[3], (BYTE_WIDTH,), jnp.float32), 0.25, 1.75),
        "w_in": draw_w_in(jax.random.fold_in(key_list[9], 71), 0),
        "attn_gain": jnp.clip(1.0 + 0.15 * jax.random.normal(key_list[5], (MODEL_WIDTH,), jnp.float32), 0.25, 1.75),
        "w_qkv": draw_w_qkv(jax.random.fold_in(key_list[9], 71), 0),
        "w_out": normal_values(key_list[7], (HEADS * HEAD_SIZE, MODEL_WIDTH), (HEADS * HEAD_SIZE) ** -0.5, 0.1875, ((0, 4),)),
        "w_down": draw_w_down(jax.random.fold_in(key_list[9], 71), 0),
    }


EPSILON = 1e-05

def rms_scale(values, gain):
    wide = values.astype(jnp.float32)
    return wide * lax.rsqrt(lax.optimization_barrier(jnp.mean(wide * wide, axis=-1, keepdims=True)) + EPSILON) * gain

def global_head(operands):
    queries, keys, values = operands
    scores = jnp.dot(queries, keys.T, preferred_element_type=jnp.float32) / math.sqrt(HEAD_SIZE)
    order = jnp.arange(PATCHES, dtype=jnp.int32)
    allowed = order[:, None] >= order[None, :]
    scores = jnp.where(allowed, scores, -jnp.inf)
    peak = lax.optimization_barrier(jnp.max(scores, axis=1, keepdims=True))
    weights = jnp.exp(scores - peak)
    total = lax.optimization_barrier(jnp.sum(weights, axis=1, keepdims=True))
    mixed = jnp.dot(weights.astype(jnp.bfloat16), values, preferred_element_type=jnp.float32)
    return (mixed / total).astype(jnp.bfloat16)

def cross_block(patch_states, operands):
    states, labels = operands
    heads = N_HEAD
    size = BYTE_WIDTH // N_HEAD
    reach = labels[:, None] - jnp.arange(WINDOW, dtype=jnp.int32)[None, :]
    valid = reach >= 0
    rows = patch_states[jnp.maximum(reach, 0).astype(jnp.int32)]
    queries = states.astype(jnp.float32).reshape(BYTES_DEV, heads, size)
    keys = rows.astype(jnp.float32).reshape(BYTES_DEV, WINDOW, heads, size)
    scores = jnp.einsum('bhc,bwhc->bhw', queries, keys, precision=lax.Precision.HIGHEST) / math.sqrt(size)
    scores = jnp.where(valid[:, None, :], scores, -jnp.inf)
    peak = lax.optimization_barrier(jnp.max(scores, axis=-1, keepdims=True))
    weights = jnp.exp(scores - peak)
    total = lax.optimization_barrier(jnp.sum(weights, axis=-1, keepdims=True))
    rounded = lax.optimization_barrier(weights.astype(jnp.bfloat16)).astype(jnp.float32)
    mixed = jnp.einsum('bhw,bwhc->bhc', rounded, keys, precision=lax.Precision.HIGHEST) / total
    return (states.astype(jnp.float32) + mixed.reshape(BYTES_DEV, BYTE_WIDTH)).astype(jnp.bfloat16)

def reference(byte_states, patch_ids, slot_patch, pool_gain, w_in, attn_gain, w_qkv, w_out, w_down):
    pooled = jax.ops.segment_sum(byte_states.astype(jnp.float32), patch_ids, num_segments=PATCHES).astype(jnp.bfloat16)
    normed = rms_scale(pooled, pool_gain).astype(jnp.bfloat16)
    embed = jnp.dot(normed, w_in, preferred_element_type=jnp.float32).astype(jnp.bfloat16)
    attn_in = rms_scale(embed, attn_gain).astype(jnp.bfloat16)
    width = HEADS * HEAD_SIZE
    projected = jnp.dot(attn_in, w_qkv.reshape(MODEL_WIDTH, 3 * width), preferred_element_type=jnp.float32).astype(jnp.bfloat16)
    split = projected.reshape(PATCHES, 3, HEADS, HEAD_SIZE).transpose(1, 2, 0, 3)
    attended = lax.map(global_head, (split[0], split[1], split[2]))
    attended = attended.transpose(1, 0, 2).reshape(PATCHES, width)
    stream = (embed.astype(jnp.float32) + jnp.dot(attended, w_out, preferred_element_type=jnp.float32)).astype(jnp.bfloat16)
    patch_out = stream[slot_patch]
    patch_states = jnp.dot(stream, w_down, preferred_element_type=jnp.float32).astype(jnp.bfloat16)
    blocks = lax.map(partial(cross_block, patch_states), (byte_states.reshape(N_SEQ, BYTES_DEV, BYTE_WIDTH), patch_ids.reshape(N_SEQ, BYTES_DEV)))
    byte_out = blocks.reshape(BYTES, BYTE_WIDTH)
    return (patch_out, byte_out)
```

```python
import functools
import math

import jax
import jax.numpy as jnp
from jax import lax
from jax.experimental import pallas as pl
from jax.experimental.pallas import tpu as pltpu
from jax.sharding import PartitionSpec as P

HEAD_SIZE = 128
WINDOW = 8
EPSILON = 1e-05
FLOOR_SCORE = -1e30
MESH = pl.DeviceIdType.MESH
F32 = jnp.float32
BF16 = jnp.bfloat16


def dot(a, b):
    return lax.dot_general(a, b, (((1,), (0,)), ((), ())), preferred_element_type=F32)


def dot_t(a, b):
    return lax.dot_general(a, b, (((1,), (1,)), ((), ())), preferred_element_type=F32)


def merge_rows(block):
    r, m, n = block.shape
    if m % 16 and r > 1:
        return block.astype(F32).reshape(r * m, n).astype(block.dtype)
    return block.reshape(r * m, n)


class SeqGather:
    def __init__(self, n_seq, src, buf, sems):
        self.n_z = n_seq // 2
        self.src, self.buf = src, buf
        self.send_z, self.send_y, self.recv, self.own = sems
        self.me = lax.axis_index("seq")
        self.z, self.y = self.me // 2, lax.rem(self.me, 2)
        self.pending = []

    def slot(self, z, y):
        return z * 2 + y

    def copy(self, src, slot, target, send_sem):
        return pltpu.make_async_remote_copy(
            src_ref=src,
            dst_ref=self.buf.at[slot],
            send_sem=send_sem,
            recv_sem=self.recv.at[slot],
            device_id={"seq": target},
            device_id_type=MESH,
        )

    def start(self):
        self.local = pltpu.make_async_copy(self.src, self.buf.at[self.me], self.own.at[0])
        self.local.start()
        c = self.copy(self.src, self.me, self.slot(self.z, 1 - self.y), self.send_y.at[0])
        c.start()
        self.pending.append(c)
        for dz in range(1, self.n_z):
            to = lax.rem(self.z + dz, self.n_z)
            c = self.copy(self.src, self.me, self.slot(to, self.y), self.send_z.at[dz])
            c.start()
            self.pending.append(c)

    def forward(self, dz):
        z = lax.rem(self.z + self.n_z - dz, self.n_z)
        slot = self.slot(z, self.y)
        c = self.copy(
            self.buf.at[slot], slot, self.slot(self.z, 1 - self.y), self.send_y.at[dz]
        )
        c.wait_recv()
        c.start()
        self.pending.append(c)

    def forward_all(self):
        for dz in range(1, self.n_z):
            self.forward(dz)

    def finish(self):
        self.local.wait()
        for z in range(self.n_z):
            slot = self.slot(z, 1 - self.y)
            self.copy(self.buf.at[slot], slot, self.me, self.send_y.at[0]).wait_recv()

    def drain(self):
        for c in self.pending:
            c.wait_send()


class HeadExchange:
    def __init__(self, n_head, buf, send, recv):
        self.n = n_head
        self.buf, self.send, self.recv = buf, send, recv
        self.me = lax.axis_index("head")
        self.pending = []

    def start(self, src_of):
        for d in range(1, self.n):
            to = lax.rem(self.me + d, self.n)
            c = pltpu.make_async_remote_copy(
                src_ref=src_of(to),
                dst_ref=self.buf.at[self.me],
                send_sem=self.send.at[d],
                recv_sem=self.recv.at[self.me],
                device_id={"head": to},
                device_id_type=MESH,
            )
            c.start()
            self.pending.append(c)

    def finish(self):
        for d in range(1, self.n):
            src = lax.rem(self.me + d, self.n)
            pltpu.make_async_remote_copy(
                src_ref=self.buf.at[src],
                dst_ref=self.buf.at[src],
                send_sem=self.send.at[d],
                recv_sem=self.recv.at[src],
                device_id={"head": src},
                device_id_type=MESH,
            ).wait_recv()

    def drain(self):
        for c in self.pending:
            c.wait_send()


def kernel(
    n_seq, n_head,
    x_ref, idr_ref, idc_ref, slotc_ref, slotr_ref, pg_ref, ag_ref,
    w_in_ref, w_qkv_ref, w_out_ref, w_down_ref,
    patch_out_ref, byte_out_ref,
    g_in, g_qkv, g_down, g_kv, g_ps, wo_g, part, rs_buf, pool_g, emb_g, att_g,
    kv_src, ps_src, down_src, down_g,
    gz, gy, gr, go, hs, hr, rss, rsr, wos,
):
    me, mh = lax.axis_index("seq"), lax.axis_index("head")
    rows = patch_out_ref.shape[0]
    width = patch_out_ref.shape[1]
    n_bytes, cross = x_ref.shape
    ratio = n_seq // n_head

    barrier = pltpu.get_barrier_semaphore()
    for d in range(1, n_seq):
        pl.semaphore_signal(
            barrier, inc=1, device_id={"seq": lax.rem(me + d, n_seq)}, device_id_type=MESH
        )
    for d in range(1, n_head):
        pl.semaphore_signal(
            barrier, inc=1, device_id={"head": lax.rem(mh + d, n_head)}, device_id_type=MESH
        )
    pl.semaphore_wait(barrier, n_seq + n_head - 2)

    def gather(i, src, buf):
        return SeqGather(n_seq, src, buf, (gz.at[i], gy.at[i], gr.at[i], go.at[i]))

    def exchange(i, buf):
        return HeadExchange(n_head, buf, hs.at[i], hr.at[i])

    in_gather = gather(0, w_in_ref, g_in)
    qkv_gather = gather(1, w_qkv_ref, g_qkv)
    down_gather = gather(2, w_down_ref, g_down)
    kv_gather = gather(3, kv_src, g_kv)
    ps_gather = gather(4, ps_src, g_ps)
    wo_x, pool_x, emb_x, att_x, down_x = (
        exchange(i, buf) for i, buf in enumerate((wo_g, pool_g, emb_g, att_g, down_g))
    )

    in_gather.start()

    def rs_copy(d):
        to = lax.rem(me + d, n_seq)
        return pltpu.make_async_remote_copy(
            src_ref=part.at[to],
            dst_ref=rs_buf.at[me],
            send_sem=rss.at[d],
            recv_sem=rsr.at[me],
            device_id={"seq": to},
            device_id_type=MESH,
        )

    def pool(to):
        match = jnp.where(slotc_ref[to] == idr_ref[...], 1.0, 0.0).astype(BF16)
        return dot(match, x_ref[...])

    def pool_step(d, carry):
        to = lax.rem(me + d, n_seq)
        part[to] = pool(to).astype(BF16)
        rs_copy(d).start()
        return carry

    lax.fori_loop(1, n_seq, pool_step, 0)
    qkv_gather.start()
    wo_x.start(lambda to: w_out_ref.at[:, pl.ds(pl.multiple_of(to * width, 128), width)])
    wo_own = pltpu.make_async_copy(
        w_out_ref.at[:, pl.ds(pl.multiple_of(mh * width, 128), width)], wo_g.at[mh], wos.at[0]
    )
    wo_own.start()
    pooled = pool(me)
    in_gather.forward_all()
    for d in range(1, n_seq):
        src = lax.rem(me + d, n_seq)
        pltpu.make_async_remote_copy(
            src_ref=rs_buf.at[src],
            dst_ref=rs_buf.at[src],
            send_sem=rss.at[d],
            recv_sem=rsr.at[src],
            device_id={"seq": src},
            device_id_type=MESH,
        ).wait_recv()
        pooled = pooled + rs_buf[src].astype(F32)
    pool_g[mh] = pooled.astype(BF16)
    pool_x.start(lambda to: pool_g.at[mh])
    pool_x.finish()

    def square_sum(buf):
        total = jnp.zeros((rows, 1), F32)
        for i in range(n_head):
            block = buf[i].astype(F32)
            total = total + jnp.sum(block * block, axis=-1, keepdims=True)
        return total

    scale = lax.rsqrt(square_sum(pool_g) / (cross * n_head) + EPSILON)
    in_gather.finish()
    embed = jnp.zeros((rows, width), F32)
    for i in range(n_head):
        normed = (pool_g[i].astype(F32) * scale * pg_ref[i]).astype(BF16)
        embed = embed + dot(normed, merge_rows(g_in[i * ratio : (i + 1) * ratio]))
    emb_g[mh] = embed.astype(BF16)
    emb_x.start(lambda to: emb_g.at[mh])
    qkv_gather.forward_all()
    down_gather.start()
    emb_x.finish()
    scale = lax.rsqrt(square_sum(emb_g) / (width * n_head) + EPSILON)
    qkv_gather.finish()
    projected = jnp.zeros((rows, w_qkv_ref.shape[1]), F32)
    for i in range(n_head):
        attn_in = (emb_g[i].astype(F32) * scale * ag_ref[i]).astype(BF16)
        projected = projected + dot(attn_in, merge_rows(g_qkv[i * ratio : (i + 1) * ratio]))
    projected = projected.astype(BF16)
    third = projected.shape[1] // 3
    kv_src[...] = projected[:, third:]
    kv_gather.start()
    queries = projected[:, :third]
    kv_gather.forward_all()
    down_gather.forward_all()
    kv_gather.finish()

    own = slotc_ref[me]
    allowed = slotr_ref[...] <= own
    for j in range(third // HEAD_SIZE):
        cols = slice(j * HEAD_SIZE, (j + 1) * HEAD_SIZE)
        keys = merge_rows(g_kv[:, :, j * HEAD_SIZE : (j + 1) * HEAD_SIZE])
        values = merge_rows(g_kv[:, :, third + j * HEAD_SIZE : third + (j + 1) * HEAD_SIZE])
        scores = dot_t(queries[:, cols], keys) * (1.0 / math.sqrt(HEAD_SIZE))
        scores = jnp.where(allowed, scores, FLOOR_SCORE)
        peak = jnp.max(scores, axis=-1, keepdims=True)
        weights = jnp.where(allowed, jnp.exp(scores - peak), 0.0)
        total = jnp.sum(weights, axis=-1, keepdims=True)
        att_g[mh, :, cols] = (dot(weights.astype(BF16), values) / total).astype(BF16)
    att_x.start(lambda to: att_g.at[mh])
    wo_own.wait()
    wo_x.finish()
    att_x.finish()
    added = jnp.zeros((rows, width), F32)
    for i in range(n_head):
        added = added + dot(att_g[i], wo_g[i])
    stream = (emb_g[mh].astype(F32) + added).astype(BF16)
    patch_out_ref[...] = stream

    down_gather.finish()
    for i in range(n_head):
        down_src[i] = dot_t(stream, merge_rows(g_down[i * ratio : (i + 1) * ratio]))
    down_x.start(lambda to: down_src.at[to])
    down_x.finish()
    states = down_src[mh]
    for d in range(1, n_head):
        states = states + down_g[lax.rem(mh + d, n_head)]
    ps_src[...] = states.astype(BF16)
    ps_gather.start()
    ps_gather.forward_all()
    ps_gather.finish()

    size = math.gcd(n_bytes, 256)

    def cross_step(t, carry):
        at = pl.ds(pl.multiple_of(t * size, size), size)
        block = x_ref[at, :]
        states = merge_rows(g_ps[...])
        ids = idc_ref[at, :]
        allowed = (slotr_ref[...] <= ids) & (slotr_ref[...] > ids - WINDOW)
        scores = dot_t(block, states) * (1.0 / math.sqrt(cross))
        scores = jnp.where(allowed, scores, FLOOR_SCORE)
        peak = jnp.max(scores, axis=-1, keepdims=True)
        weights = jnp.where(allowed, jnp.exp(scores - peak), 0.0)
        total = jnp.sum(weights, axis=-1, keepdims=True)
        mixed = dot(weights.astype(BF16), states) / total
        byte_out_ref[at, :] = (block.astype(F32) + mixed).astype(BF16)
        return carry

    lax.fori_loop(0, n_bytes // size, cross_step, 0)

    for g in (in_gather, qkv_gather, down_gather, kv_gather, ps_gather):
        g.drain()
    for x in (wo_x, pool_x, emb_x, att_x, down_x):
        x.drain()
    for d in range(1, n_seq):
        rs_copy(d).wait_send()


def body(byte_states, patch_ids, slot_patch, pool_gain, w_in, attn_gain, w_qkv, w_out, w_down):
    n_seq, n_head = lax.axis_size("seq"), lax.axis_size("head")
    rows = slot_patch.shape[0] // n_seq
    n_bytes, cross = byte_states.shape
    width = w_in.shape[1]
    qkv = w_qkv.reshape(w_qkv.shape[0], -1)
    third = w_qkv.shape[2]
    down = w_down.T
    n_z = n_seq // 2
    vmem = pl.BlockSpec(memory_space=pltpu.VMEM)
    anywhere = pl.BlockSpec(memory_space=pl.ANY)
    dma = pltpu.SemaphoreType.DMA
    return pl.pallas_call(
        functools.partial(kernel, n_seq, n_head),
        out_shape=(
            jax.ShapeDtypeStruct((rows, width), BF16),
            jax.ShapeDtypeStruct((n_bytes, cross), BF16),
        ),
        in_specs=[vmem] * 7 + [anywhere] * 4,
        out_specs=(vmem, vmem),
        scratch_shapes=[
            pltpu.VMEM((n_seq,) + w_in.shape, BF16),
            pltpu.VMEM((n_seq,) + qkv.shape, BF16),
            pltpu.VMEM((n_seq,) + down.shape, BF16),
            pltpu.VMEM((n_seq, rows, 2 * third), BF16),
            pltpu.VMEM((n_seq, rows, cross), BF16),
            pltpu.VMEM((n_head, w_out.shape[0], width), BF16),
            pltpu.VMEM((n_seq, rows, cross), BF16),
            pltpu.VMEM((n_seq, rows, cross), BF16),
            pltpu.VMEM((n_head, rows, cross), BF16),
            pltpu.VMEM((n_head, rows, width), BF16),
            pltpu.VMEM((n_head, rows, third), BF16),
            pltpu.VMEM((rows, 2 * third), BF16),
            pltpu.VMEM((rows, cross), BF16),
            pltpu.VMEM((n_head, rows, cross), F32),
            pltpu.VMEM((n_head, rows, cross), F32),
            dma((5, n_z)),
            dma((5, n_z)),
            dma((5, n_seq)),
            dma((5, 1)),
            dma((5, n_head)),
            dma((5, n_head)),
            dma((n_seq,)),
            dma((n_seq,)),
            dma((1,)),
        ],
        compiler_params=pltpu.CompilerParams(
            collective_id=0, has_side_effects=True, vmem_limit_bytes=56 * 1024 * 1024
        ),
    )(
        byte_states,
        patch_ids.reshape(1, -1),
        patch_ids.reshape(-1, 1),
        slot_patch.reshape(n_seq, rows, 1),
        slot_patch.reshape(1, -1),
        pool_gain.reshape(n_head, 1, cross),
        attn_gain.reshape(n_head, 1, width),
        w_in,
        qkv,
        w_out,
        down,
    )


def solution(mesh):
    placed = (
        P("seq", "head"),
        P("seq"),
        P(),
        P(),
        P("seq", "head"),
        P(),
        P("seq", None, "head"),
        P("head", None),
        P("head", "seq"),
    )
    return jax.shard_map(
        body,
        mesh=mesh,
        in_specs=placed,
        out_specs=(P("seq", "head"), P("seq", "head")),
        check_vma=False,
    )
```

```python
import functools
import math

import jax
import jax.numpy as jnp
from jax import lax
from jax.experimental import pallas as pl
from jax.experimental.pallas import tpu as pltpu
from jax.sharding import PartitionSpec as P

HEAD_SIZE = 128
WINDOW = 8
EPSILON = 1e-05
FLOOR_SCORE = -1e30
MESH = pl.DeviceIdType.MESH
F32 = jnp.float32
BF16 = jnp.bfloat16


def dot(a, b):
    return lax.dot_general(a, b, (((1,), (0,)), ((), ())), preferred_element_type=F32)


def dot_t(a, b):
    return lax.dot_general(a, b, (((1,), (1,)), ((), ())), preferred_element_type=F32)


def lanes(n):
    return -(-n // 128) * 128


def merge_rows(block):
    r, m, n = block.shape
    if m % 16 and r > 1:
        return block.astype(F32).reshape(r * m, n).astype(block.dtype)
    return block.reshape(r * m, n)


class Gather:
    def __init__(self, axis, src, buf, sems):
        self.axis = axis
        self.n_z = lax.axis_size(axis) // 2
        self.src, self.buf = src, buf
        self.send_z, self.send_y, self.recv, self.own = sems
        self.me = lax.axis_index(axis)
        self.z, self.y = self.me // 2, lax.rem(self.me, 2)
        self.pending = []

    def slot(self, z, y):
        return z * 2 + y

    def copy(self, src, slot, target, send_sem):
        return pltpu.make_async_remote_copy(
            src_ref=src,
            dst_ref=self.buf.at[slot],
            send_sem=send_sem,
            recv_sem=self.recv.at[slot],
            device_id={self.axis: target},
            device_id_type=MESH,
        )

    def start(self):
        self.local = pltpu.make_async_copy(self.src, self.buf.at[self.me], self.own.at[0])
        self.local.start()
        for dz in range(1, self.n_z):
            to = lax.rem(self.z + dz, self.n_z)
            c = self.copy(self.src, self.me, self.slot(to, self.y), self.send_z.at[dz])
            c.start()
            self.pending.append(c)
        c = self.copy(self.src, self.me, self.slot(self.z, 1 - self.y), self.send_y.at[0])
        c.start()
        self.pending.append(c)

    def forward_all(self):
        for dz in range(1, self.n_z):
            z = lax.rem(self.z + self.n_z - dz, self.n_z)
            slot = self.slot(z, self.y)
            c = self.copy(
                self.buf.at[slot], slot, self.slot(self.z, 1 - self.y), self.send_y.at[dz]
            )
            c.wait_recv()
            c.start()
            self.pending.append(c)

    def finish(self):
        self.local.wait()
        for z in range(self.n_z):
            slot = self.slot(z, 1 - self.y)
            self.copy(self.buf.at[slot], slot, self.me, self.send_y.at[0]).wait_recv()

    def drain(self):
        for c in self.pending:
            c.wait_send()


class Exchange:
    def __init__(self, n, me, device, buf, send, recv):
        self.n, self.me, self.device = n, me, device
        self.buf, self.send, self.recv = buf, send, recv
        self.pending = []

    def send_to(self, src, d):
        to = lax.rem(self.me + d, self.n)
        c = pltpu.make_async_remote_copy(
            src_ref=src,
            dst_ref=self.buf.at[self.me],
            send_sem=self.send.at[d],
            recv_sem=self.recv.at[self.me],
            device_id=self.device(to),
            device_id_type=MESH,
        )
        c.start()
        self.pending.append(c)

    def start(self, src_of):
        for d in range(1, self.n):
            self.send_to(src_of(lax.rem(self.me + d, self.n)), d)

    def wait_from(self, src, d):
        pltpu.make_async_remote_copy(
            src_ref=self.buf.at[src],
            dst_ref=self.buf.at[src],
            send_sem=self.send.at[d],
            recv_sem=self.recv.at[src],
            device_id=self.device(src),
            device_id_type=MESH,
        ).wait_recv()

    def finish(self):
        for d in range(1, self.n):
            self.wait_from(lax.rem(self.me + d, self.n), d)

    def drain(self):
        for c in self.pending:
            c.wait_send()


def kernel(
    n_seq, n_head,
    x_ref, small_ref, ag_ref,
    w_in_ref, w_qkv_ref, w_out_ref, w_down_ref,
    patch_out_ref, byte_out_ref,
    g_in, g_qkv, g_down, g_kv, g_ps, wo_g, part, rs_buf, pool_g, emb_g, att_g,
    kv_src, ps_src, down_src, down_g, slotc_ref, pool_src, emb_src, att_src,
    a_src, a_buf, prj_src, prj_buf,
    gz, gy, gr, go, jz, jy, jr, jo, hs, hr, zs, zr, rss, rsr, wos, qs,
):
    me, mh = lax.axis_index("seq"), lax.axis_index("head")
    rows = patch_out_ref.shape[0]
    width = patch_out_ref.shape[1]
    cross, n_bytes = x_ref.shape
    n_z = n_seq // 2
    z, y = me // 2, lax.rem(me, 2)
    n_patches = n_seq * rows
    third = w_qkv_ref.shape[2]
    ratio = n_seq // n_head

    barrier = pltpu.get_barrier_semaphore()
    for d in range(1, n_seq):
        pl.semaphore_signal(
            barrier, inc=1, device_id={"seq": lax.rem(me + d, n_seq)}, device_id_type=MESH
        )
    for d in range(1, n_head):
        pl.semaphore_signal(
            barrier, inc=1, device_id={"head": lax.rem(mh + d, n_head)}, device_id_type=MESH
        )
    pl.semaphore_wait(barrier, n_seq + n_head - 2)

    def gather(i, src, buf):
        return Gather("seq", src, buf, (gz.at[i], gy.at[i], gr.at[i], go.at[i]))

    def head_gather(i, src, buf):
        return Gather("head", src, buf, (jz.at[i], jy.at[i], jr.at[i], jo.at[i]))

    def exchange(i, buf):
        return Exchange(n_head, mh, lambda to: {"head": to}, buf, hs.at[i], hr.at[i])

    def z_exchange(i, buf):
        return Exchange(n_z, z, lambda to: {"seq": to * 2 + y}, buf, zs.at[i], zr.at[i])

    in_gather = gather(0, w_in_ref, g_in)
    down_gather = gather(1, w_down_ref, g_down)
    kv_gather = gather(2, kv_src, g_kv)
    ps_gather = gather(3, ps_src, g_ps)
    pool_x = head_gather(0, pool_src, pool_g)
    emb_x = head_gather(1, emb_src, emb_g)
    att_x = head_gather(2, att_src, att_g)
    wo_x, down_x = exchange(0, wo_g), exchange(1, down_g)
    a_x, prj_x = z_exchange(0, a_buf), z_exchange(1, prj_buf)
    ids = small_ref[:, :n_bytes]
    slotr = small_ref[:, n_bytes : n_bytes + n_patches]

    in_gather.start()
    wo_x.start(lambda to: w_out_ref.at[:, pl.ds(pl.multiple_of(to * width, 128), width)])
    wo_own = pltpu.make_async_copy(
        w_out_ref.at[:, pl.ds(pl.multiple_of(mh * width, 128), width)], wo_g.at[mh], wos.at[0]
    )
    wo_own.start()
    qkv_own = pltpu.make_async_copy(w_qkv_ref, g_qkv.at[y], qs.at[0])
    qkv_own.start()

    down = lax.broadcasted_iota(jnp.int32, (rows, n_patches), 0)
    along = lax.broadcasted_iota(jnp.int32, (rows, n_patches), 1)

    def slot_step(i, carry):
        slotc_ref[i] = jnp.sum(
            jnp.where(down + i * rows == along, slotr, 0.0), axis=-1, keepdims=True
        )
        return carry

    lax.fori_loop(0, n_seq, slot_step, 0)

    def rs_copy(d):
        to = lax.rem(me + d, n_seq)
        return pltpu.make_async_remote_copy(
            src_ref=part.at[to],
            dst_ref=rs_buf.at[me],
            send_sem=rss.at[d],
            recv_sem=rsr.at[me],
            device_id={"seq": to},
            device_id_type=MESH,
        )

    def pool(to):
        match = jnp.where(slotc_ref[to] == ids, 1.0, 0.0).astype(BF16)
        return dot_t(match, x_ref[...])

    def pool_step(d, carry):
        to = lax.rem(me + d, n_seq)
        part[to] = pool(to).astype(BF16)
        rs_copy(d).start()
        return carry

    lax.fori_loop(1, n_seq, pool_step, 0)
    pooled = pool(me)
    in_gather.forward_all()
    qkv_copy = pltpu.make_async_remote_copy(
        src_ref=w_qkv_ref,
        dst_ref=g_qkv.at[y],
        send_sem=qs.at[1],
        recv_sem=qs.at[2],
        device_id={"seq": z * 2 + 1 - y},
        device_id_type=MESH,
    )
    qkv_copy.start()
    for d in range(1, n_seq):
        src = lax.rem(me + d, n_seq)
        pltpu.make_async_remote_copy(
            src_ref=rs_buf.at[src],
            dst_ref=rs_buf.at[src],
            send_sem=rss.at[d],
            recv_sem=rsr.at[src],
            device_id={"seq": src},
            device_id_type=MESH,
        ).wait_recv()
        pooled = pooled + rs_buf[src].astype(F32)
    pool_src[...] = pooled.astype(BF16)
    pool_x.start()
    pool_x.forward_all()
    pool_x.finish()
    down_gather.start()

    def square_sum(buf):
        total = jnp.zeros((rows, 1), F32)
        for i in range(n_head):
            block = buf[i].astype(F32)
            total = total + jnp.sum(block * block, axis=-1, keepdims=True)
        return total

    scale = lax.rsqrt(square_sum(pool_g) / (cross * n_head) + EPSILON)
    in_gather.finish()
    embed = jnp.zeros((rows, width), F32)
    for i in range(n_head):
        at = n_bytes + n_patches + i * lanes(cross)
        gain = small_ref[:, at : at + cross]
        normed = (pool_g[i].astype(F32) * scale * gain).astype(BF16)
        embed = embed + dot(normed, merge_rows(g_in[i * ratio : (i + 1) * ratio]))
    emb_src[...] = embed.astype(BF16)
    emb_x.start()
    emb_x.forward_all()
    emb_x.finish()
    scale = lax.rsqrt(square_sum(emb_g) / (width * n_head) + EPSILON)
    for d in list(range(1, n_z)) + [0]:
        to = lax.rem(z + d, n_z)
        a_src[to] = (emb_g[to].astype(F32) * scale * ag_ref[to]).astype(BF16)
        if d:
            a_x.send_to(a_src.at[to], d)

    def project(block):
        return [dot(block, merge_rows(g_qkv[:, j])) for j in range(3)]

    qkv_own.wait()
    qkv_copy.wait_recv()
    projected = project(a_src[z])
    down_gather.forward_all()
    for d in range(n_z - 1, 0, -1):
        source = lax.rem(z + d, n_z)
        a_x.wait_from(source, d)
        for j, piece in enumerate(project(a_buf[source])):
            prj_src[source, :, j * third : (j + 1) * third] = piece.astype(BF16)
        prj_x.send_to(prj_src.at[source], d)
    prj_x.finish()
    for d in range(1, n_z):
        source = lax.rem(z + d, n_z)
        projected = [
            piece + prj_buf[source, :, j * third : (j + 1) * third].astype(F32)
            for j, piece in enumerate(projected)
        ]
    queries = projected[0].astype(BF16)
    kv_src[:, :third] = projected[1].astype(BF16)
    kv_src[:, third:] = projected[2].astype(BF16)
    kv_gather.start()
    kv_gather.forward_all()
    kv_gather.finish()

    own = slotc_ref[me]
    allowed = slotr <= own
    for j in range(third // HEAD_SIZE):
        cols = slice(j * HEAD_SIZE, (j + 1) * HEAD_SIZE)
        keys = merge_rows(g_kv[:, :, j * HEAD_SIZE : (j + 1) * HEAD_SIZE])
        values = merge_rows(g_kv[:, :, third + j * HEAD_SIZE : third + (j + 1) * HEAD_SIZE])
        scores = dot_t(queries[:, cols], keys) * (1.0 / math.sqrt(HEAD_SIZE))
        scores = jnp.where(allowed, scores, FLOOR_SCORE)
        peak = jnp.max(scores, axis=-1, keepdims=True)
        weights = jnp.where(allowed, jnp.exp(scores - peak), 0.0)
        total = jnp.sum(weights, axis=-1, keepdims=True)
        att_src[:, cols] = (dot(weights.astype(BF16), values) / total).astype(BF16)
    att_x.start()
    att_x.forward_all()
    wo_own.wait()
    wo_x.finish()
    att_x.finish()
    added = jnp.zeros((rows, width), F32)
    for i in range(n_head):
        added = added + dot(att_g[i], wo_g[i])
    stream = (emb_src[...].astype(F32) + added).astype(BF16)
    patch_out_ref[...] = stream

    down_gather.finish()

    def down_part(i):
        pieces = [dot_t(stream, g_down[i * ratio + j]) for j in range(ratio)]
        return pieces[0] if ratio == 1 else jnp.concatenate(pieces, axis=-1)

    for d in range(1, n_head):
        to = lax.rem(mh + d, n_head)
        down_src[to] = down_part(to).astype(BF16)
        down_x.send_to(down_src.at[to], d)
    states = down_part(mh)
    down_x.finish()
    for d in range(1, n_head):
        states = states + down_g[lax.rem(mh + d, n_head)].astype(F32)
    ps_src[...] = states.astype(BF16)
    ps_gather.start()
    ps_gather.forward_all()
    ps_gather.finish()

    size = math.gcd(n_bytes, 256)

    slots = slotc_ref[...].reshape(n_patches, 1)

    def cross_step(t, carry):
        at = pl.ds(pl.multiple_of(t * size, 128), size)
        block = x_ref[:, at]
        states = merge_rows(g_ps[...])
        labels = small_ref[:, at]
        allowed = (slots <= labels) & (slots > labels - WINDOW)
        scores = dot(states, block) * (1.0 / math.sqrt(cross))
        scores = jnp.where(allowed, scores, FLOOR_SCORE)
        peak = jnp.max(scores, axis=0, keepdims=True)
        weights = jnp.where(allowed, jnp.exp(scores - peak), 0.0)
        total = jnp.sum(weights, axis=0, keepdims=True)
        mixed = lax.dot_general(
            states, weights.astype(BF16), (((0,), (0,)), ((), ())), preferred_element_type=F32
        )
        byte_out_ref[:, at] = (block.astype(F32) + mixed / total).astype(BF16)
        return carry

    lax.fori_loop(0, n_bytes // size, cross_step, 0)

    qkv_copy.wait_send()
    for g in (in_gather, down_gather, kv_gather, ps_gather, pool_x, emb_x, att_x):
        g.drain()
    for x in (wo_x, down_x, a_x, prj_x):
        x.drain()
    for d in range(1, n_seq):
        rs_copy(d).wait_send()


def body(byte_states, patch_ids, slot_patch, pool_gain, w_in, attn_gain, w_qkv, w_out, w_down):
    n_seq, n_head = lax.axis_size("seq"), lax.axis_size("head")
    rows = slot_patch.shape[0] // n_seq
    n_bytes, cross = byte_states.shape
    width = w_in.shape[1]
    qkv = w_qkv.transpose(1, 0, 2)
    third = w_qkv.shape[2]
    down = w_down.T
    n_z = n_seq // 2
    gains = jnp.pad(
        pool_gain.reshape(n_head, cross), ((0, 0), (0, lanes(cross) - cross))
    ).reshape(-1)
    small = jnp.concatenate([patch_ids.astype(F32), slot_patch.astype(F32), gains])
    small = jnp.pad(small, (0, -small.shape[0] % 1024)).reshape(1, -1)
    vmem = pl.BlockSpec(memory_space=pltpu.VMEM)
    anywhere = pl.BlockSpec(memory_space=pl.ANY)
    dma = pltpu.SemaphoreType.DMA
    n_x = n_head // 2
    stream, byte_out = pl.pallas_call(
        functools.partial(kernel, n_seq, n_head),
        out_shape=(
            jax.ShapeDtypeStruct((rows, width), BF16),
            jax.ShapeDtypeStruct((cross, n_bytes), BF16),
        ),
        in_specs=[vmem] * 3 + [anywhere] * 4,
        out_specs=(vmem, vmem),
        scratch_shapes=[
            pltpu.VMEM((n_seq,) + w_in.shape, BF16),
            pltpu.VMEM((2,) + qkv.shape, BF16),
            pltpu.VMEM((n_seq,) + down.shape, BF16),
            pltpu.VMEM((n_seq, rows, 2 * third), BF16),
            pltpu.VMEM((n_seq, rows, cross), BF16),
            pltpu.VMEM((n_head, w_out.shape[0], width), BF16),
            pltpu.VMEM((n_seq, rows, cross), BF16),
            pltpu.VMEM((n_seq, rows, cross), BF16),
            pltpu.VMEM((n_head, rows, cross), BF16),
            pltpu.VMEM((n_head, rows, width), BF16),
            pltpu.VMEM((n_head, rows, third), BF16),
            pltpu.VMEM((rows, 2 * third), BF16),
            pltpu.VMEM((rows, cross), BF16),
            pltpu.VMEM((n_head, rows, cross), BF16),
            pltpu.VMEM((n_head, rows, cross), BF16),
            pltpu.VMEM((n_seq, rows, 1), F32),
            pltpu.VMEM((rows, cross), BF16),
            pltpu.VMEM((rows, width), BF16),
            pltpu.VMEM((rows, third), BF16),
            pltpu.VMEM((n_z, rows, width), BF16),
            pltpu.VMEM((n_z, rows, width), BF16),
            pltpu.VMEM((n_z, rows, 3 * third), BF16),
            pltpu.VMEM((n_z, rows, 3 * third), BF16),
            dma((4, n_z)),
            dma((4, n_z)),
            dma((4, n_seq)),
            dma((4, 1)),
            dma((3, n_x)),
            dma((3, n_x)),
            dma((3, n_head)),
            dma((3, 1)),
            dma((2, n_head)),
            dma((2, n_head)),
            dma((2, n_z)),
            dma((2, n_z)),
            dma((n_seq,)),
            dma((n_seq,)),
            dma((1,)),
            dma((3,)),
        ],
        compiler_params=pltpu.CompilerParams(
            collective_id=0, has_side_effects=True, vmem_limit_bytes=56 * 1024 * 1024
        ),
    )(
        byte_states.T,
        small,
        attn_gain.reshape(n_head, 1, width),
        w_in,
        qkv,
        w_out,
        down,
    )
    return stream, byte_out.T


def solution(mesh):
    placed = (
        P("seq", "head"),
        P("seq"),
        P(),
        P(),
        P("seq", "head"),
        P(),
        P("seq", None, "head"),
        P("head", None),
        P("head", "seq"),
    )
    return jax.shard_map(
        body,
        mesh=mesh,
        in_specs=placed,
        out_specs=(P("seq", "head"), P("seq", "head")),
        check_vma=False,
    )
```

```python
import functools
import math

import jax
import jax.numpy as jnp
from jax import lax
from jax.experimental import pallas as pl
from jax.experimental.pallas import tpu as pltpu
from jax.sharding import PartitionSpec as P

HEAD_SIZE = 128
WINDOW = 8
EPSILON = 1e-05
FLOOR_SCORE = -1e30
MESH = pl.DeviceIdType.MESH
F32 = jnp.float32
BF16 = jnp.bfloat16


def dot(a, b):
    return lax.dot_general(a, b, (((1,), (0,)), ((), ())), preferred_element_type=F32)


def dot_t(a, b):
    return lax.dot_general(a, b, (((1,), (1,)), ((), ())), preferred_element_type=F32)


def lanes(n):
    return -(-n // 128) * 128


def merge_rows(block):
    r, m, n = block.shape
    if m % 16 and r > 1:
        return block.astype(F32).reshape(r * m, n).astype(block.dtype)
    return block.reshape(r * m, n)


class Gather:
    def __init__(self, axis, src, buf, sems):
        self.axis = axis
        self.n_z = lax.axis_size(axis) // 2
        self.src, self.buf = src, buf
        self.send_z, self.send_y, self.recv, self.own = sems
        self.me = lax.axis_index(axis)
        self.z, self.y = self.me // 2, lax.rem(self.me, 2)
        self.pending = []

    def slot(self, z, y):
        return z * 2 + y

    def copy(self, src, slot, target, send_sem):
        return pltpu.make_async_remote_copy(
            src_ref=src,
            dst_ref=self.buf.at[slot],
            send_sem=send_sem,
            recv_sem=self.recv.at[slot],
            device_id={self.axis: target},
            device_id_type=MESH,
        )

    def start(self):
        self.local = pltpu.make_async_copy(self.src, self.buf.at[self.me], self.own.at[0])
        self.local.start()
        for dz in range(1, self.n_z):
            to = lax.rem(self.z + dz, self.n_z)
            c = self.copy(self.src, self.me, self.slot(to, self.y), self.send_z.at[dz])
            c.start()
            self.pending.append(c)
        c = self.copy(self.src, self.me, self.slot(self.z, 1 - self.y), self.send_y.at[0])
        c.start()
        self.pending.append(c)

    def forward_all(self):
        for dz in range(1, self.n_z):
            z = lax.rem(self.z + self.n_z - dz, self.n_z)
            slot = self.slot(z, self.y)
            c = self.copy(
                self.buf.at[slot], slot, self.slot(self.z, 1 - self.y), self.send_y.at[dz]
            )
            c.wait_recv()
            c.start()
            self.pending.append(c)

    def finish(self):
        self.local.wait()
        for z in range(self.n_z):
            slot = self.slot(z, 1 - self.y)
            self.copy(self.buf.at[slot], slot, self.me, self.send_y.at[0]).wait_recv()

    def drain(self):
        for c in self.pending:
            c.wait_send()


class Exchange:
    def __init__(self, n, me, device, buf, send, recv):
        self.n, self.me, self.device = n, me, device
        self.buf, self.send, self.recv = buf, send, recv
        self.pending = []

    def send_to(self, src, d):
        to = lax.rem(self.me + d, self.n)
        c = pltpu.make_async_remote_copy(
            src_ref=src,
            dst_ref=self.buf.at[self.me],
            send_sem=self.send.at[d],
            recv_sem=self.recv.at[self.me],
            device_id=self.device(to),
            device_id_type=MESH,
        )
        c.start()
        self.pending.append(c)

    def start(self, src_of):
        for d in range(1, self.n):
            self.send_to(src_of(lax.rem(self.me + d, self.n)), d)

    def wait_from(self, src, d):
        pltpu.make_async_remote_copy(
            src_ref=self.buf.at[src],
            dst_ref=self.buf.at[src],
            send_sem=self.send.at[d],
            recv_sem=self.recv.at[src],
            device_id=self.device(src),
            device_id_type=MESH,
        ).wait_recv()

    def finish(self):
        for d in range(1, self.n):
            self.wait_from(lax.rem(self.me + d, self.n), d)

    def drain(self):
        for c in self.pending:
            c.wait_send()


def kernel(
    n_seq, n_head,
    x_ref, small_ref, ag_ref,
    w_in_ref, w_qkv_ref, w_out_ref, w_down_ref,
    patch_out_ref, byte_out_ref,
    g_in, g_qkv, g_down, g_kv, g_ps, wo_g, part, rs_buf, pool_g, emb_g, att_g,
    kv_src, ps_src, down_src, down_g, slotc_ref, pool_src, emb_src, att_src,
    a_src, a_buf, prj_src, prj_buf,
    gz, gy, gr, go, jz, jy, jr, jo, hs, hr, zs, zr, rss, rsr, wos, qs, shs,
):
    me, mh = lax.axis_index("seq"), lax.axis_index("head")
    rows = patch_out_ref.shape[0]
    width = patch_out_ref.shape[1]
    cross, n_bytes = x_ref.shape
    n_z = n_seq // 2
    z, y, core = me // 2, lax.rem(me, 2), lax.rem(mh, 2)
    n_patches = n_seq * rows
    third = w_qkv_ref.shape[2]
    ratio = n_seq // n_head

    barrier = pltpu.get_barrier_semaphore()
    for d in range(1, n_seq):
        pl.semaphore_signal(
            barrier, inc=1, device_id={"seq": lax.rem(me + d, n_seq)}, device_id_type=MESH
        )
    for d in range(1, n_head):
        pl.semaphore_signal(
            barrier, inc=1, device_id={"head": lax.rem(mh + d, n_head)}, device_id_type=MESH
        )
    pl.semaphore_wait(barrier, n_seq + n_head - 2)

    def gather(i, src, buf):
        return Gather("seq", src, buf, (gz.at[i], gy.at[i], gr.at[i], go.at[i]))

    def head_gather(i, src, buf):
        return Gather("head", src, buf, (jz.at[i], jy.at[i], jr.at[i], jo.at[i]))

    def exchange(i, buf):
        return Exchange(n_head, mh, lambda to: {"head": to}, buf, hs.at[i], hr.at[i])

    def z_exchange(i, buf):
        return Exchange(n_z, z, lambda to: {"seq": to * 2 + y}, buf, zs.at[i], zr.at[i])

    in_gather = gather(0, w_in_ref, g_in)
    down_gather = gather(1, w_down_ref, g_down)
    kv_gather = gather(2, kv_src, g_kv)
    ps_gather = gather(3, ps_src, g_ps)
    pool_x = head_gather(0, pool_src, pool_g)
    emb_x = head_gather(1, emb_src, emb_g)
    att_x = head_gather(2, att_src, att_g)
    wo_x, down_x = exchange(0, wo_g), exchange(1, down_g)
    a_x, prj_x = z_exchange(0, a_buf), z_exchange(1, prj_buf)
    ids = small_ref[:, :n_bytes]
    slotr = small_ref[:, n_bytes : n_bytes + n_patches]

    in_gather.start()
    wo_x.start(lambda to: w_out_ref.at[:, pl.ds(pl.multiple_of(to * width, 128), width)])
    wo_own = pltpu.make_async_copy(
        w_out_ref.at[:, pl.ds(pl.multiple_of(mh * width, 128), width)], wo_g.at[mh], wos.at[0]
    )
    wo_own.start()
    qkv_own = pltpu.make_async_copy(w_qkv_ref, g_qkv.at[y], qs.at[0])
    qkv_own.start()

    down = lax.broadcasted_iota(jnp.int32, (rows, n_patches), 0)
    along = lax.broadcasted_iota(jnp.int32, (rows, n_patches), 1)

    def slot_step(i, carry):
        slotc_ref[i] = jnp.sum(
            jnp.where(down + i * rows == along, slotr, 0.0), axis=-1, keepdims=True
        )
        return carry

    lax.fori_loop(0, n_seq, slot_step, 0)

    def rs_copy(d):
        to = lax.rem(me + d, n_seq)
        return pltpu.make_async_remote_copy(
            src_ref=part.at[to],
            dst_ref=rs_buf.at[me],
            send_sem=rss.at[d],
            recv_sem=rsr.at[me],
            device_id={"seq": to},
            device_id_type=MESH,
        )

    def pool(to):
        match = jnp.where(slotc_ref[to] == ids, 1.0, 0.0).astype(BF16)
        return dot_t(match, x_ref[...])

    def pool_step(d, carry):
        to = lax.rem(me + d, n_seq)
        part[to] = pool(to).astype(BF16)
        rs_copy(d).start()
        return carry

    lax.fori_loop(1, n_seq, pool_step, 0)
    pooled = pool(me)
    in_gather.forward_all()
    qkv_copy = pltpu.make_async_remote_copy(
        src_ref=w_qkv_ref,
        dst_ref=g_qkv.at[y],
        send_sem=qs.at[1],
        recv_sem=qs.at[2],
        device_id={"seq": z * 2 + 1 - y},
        device_id_type=MESH,
    )
    qkv_copy.start()
    down_gather.start()
    for d in range(1, n_seq):
        src = lax.rem(me + d, n_seq)
        pltpu.make_async_remote_copy(
            src_ref=rs_buf.at[src],
            dst_ref=rs_buf.at[src],
            send_sem=rss.at[d],
            recv_sem=rsr.at[src],
            device_id={"seq": src},
            device_id_type=MESH,
        ).wait_recv()
        pooled = pooled + rs_buf[src].astype(F32)
    pool_src[...] = pooled.astype(BF16)
    pool_x.start()
    pool_x.forward_all()
    pool_x.finish()

    def square_sum(buf):
        total = jnp.zeros((rows, 1), F32)
        for i in range(n_head):
            block = buf[i].astype(F32)
            total = total + jnp.sum(block * block, axis=-1, keepdims=True)
        return total

    scale = lax.rsqrt(square_sum(pool_g) / (cross * n_head) + EPSILON)
    in_gather.finish()
    embed = jnp.zeros((rows, width), F32)
    for i in range(n_head):
        at = n_bytes + n_patches + i * lanes(cross)
        gain = small_ref[:, at : at + cross]
        normed = (pool_g[i].astype(F32) * scale * gain).astype(BF16)
        embed = embed + dot(normed, merge_rows(g_in[i * ratio : (i + 1) * ratio]))
    emb_src[...] = embed.astype(BF16)
    emb_x.start()
    emb_x.forward_all()
    emb_x.finish()
    scale = lax.rsqrt(square_sum(emb_g) / (width * n_head) + EPSILON)
    for d in list(range(1, n_z)) + [0]:
        to = lax.rem(z + d, n_z)
        a_src[to] = (emb_g[to].astype(F32) * scale * ag_ref[to]).astype(BF16)
        if d:

            @pl.when(core == d % 2)
            def send(to=to, d=d):
                a_x.send_to(a_src.at[to], d)

    def share(source, d):
        return pltpu.make_async_remote_copy(
            src_ref=a_buf.at[source],
            dst_ref=a_buf.at[source],
            send_sem=shs.at[d],
            recv_sem=zr.at[0, source],
            device_id={"head": mh + 1 - 2 * core},
            device_id_type=MESH,
        )

    def project(block):
        return [dot(block, merge_rows(g_qkv[:, j])) for j in range(3)]

    qkv_own.wait()
    qkv_copy.wait_recv()
    projected = project(a_src[z])
    down_gather.forward_all()
    for d in range(1, n_z):
        source = lax.rem(z + n_z - d, n_z)
        a_x.wait_from(source, d)

        @pl.when(core == d % 2)
        def pass_on(source=source, d=d):
            share(source, d).start()

        for j, piece in enumerate(project(a_buf[source])):
            prj_src[source, :, j * third : (j + 1) * third] = piece.astype(BF16)
        prj_x.send_to(prj_src.at[source], n_z - d)
    prj_x.finish()
    for d in range(1, n_z):
        source = lax.rem(z + d, n_z)
        projected = [
            piece + prj_buf[source, :, j * third : (j + 1) * third].astype(F32)
            for j, piece in enumerate(projected)
        ]
    queries = projected[0].astype(BF16)
    kv_src[:, :third] = projected[1].astype(BF16)
    kv_src[:, third:] = projected[2].astype(BF16)
    kv_gather.start()
    kv_gather.forward_all()
    kv_gather.finish()

    own = slotc_ref[me]
    allowed = slotr <= own
    for j in range(third // HEAD_SIZE):
        cols = slice(j * HEAD_SIZE, (j + 1) * HEAD_SIZE)
        keys = merge_rows(g_kv[:, :, j * HEAD_SIZE : (j + 1) * HEAD_SIZE])
        values = merge_rows(g_kv[:, :, third + j * HEAD_SIZE : third + (j + 1) * HEAD_SIZE])
        scores = dot_t(queries[:, cols], keys) * (1.0 / math.sqrt(HEAD_SIZE))
        scores = jnp.where(allowed, scores, FLOOR_SCORE)
        peak = jnp.max(scores, axis=-1, keepdims=True)
        weights = jnp.where(allowed, jnp.exp(scores - peak), 0.0)
        total = jnp.sum(weights, axis=-1, keepdims=True)
        att_src[:, cols] = (dot(weights.astype(BF16), values) / total).astype(BF16)
    att_x.start()
    att_x.forward_all()
    wo_own.wait()
    wo_x.finish()
    att_x.finish()
    added = jnp.zeros((rows, width), F32)
    for i in range(n_head):
        added = added + dot(att_g[i], wo_g[i])
    stream = (emb_src[...].astype(F32) + added).astype(BF16)
    patch_out_ref[...] = stream

    down_gather.finish()

    def down_part(i):
        pieces = [dot_t(stream, g_down[i * ratio + j]) for j in range(ratio)]
        return pieces[0] if ratio == 1 else jnp.concatenate(pieces, axis=-1)

    for d in range(1, n_head):
        to = lax.rem(mh + d, n_head)
        down_src[to] = down_part(to).astype(BF16)
        down_x.send_to(down_src.at[to], d)
    states = down_part(mh)
    down_x.finish()
    for d in range(1, n_head):
        states = states + down_g[lax.rem(mh + d, n_head)].astype(F32)
    ps_src[...] = states.astype(BF16)
    ps_gather.start()
    ps_gather.forward_all()
    ps_gather.finish()

    size = math.gcd(n_bytes, 256)

    slots = slotc_ref[...].reshape(n_patches, 1)

    def cross_step(t, carry):
        at = pl.ds(pl.multiple_of(t * size, 128), size)
        block = x_ref[:, at]
        states = merge_rows(g_ps[...])
        labels = small_ref[:, at]
        allowed = (slots <= labels) & (slots > labels - WINDOW)
        scores = dot(states, block) * (1.0 / math.sqrt(cross))
        scores = jnp.where(allowed, scores, FLOOR_SCORE)
        peak = jnp.max(scores, axis=0, keepdims=True)
        weights = jnp.where(allowed, jnp.exp(scores - peak), 0.0)
        total = jnp.sum(weights, axis=0, keepdims=True)
        mixed = lax.dot_general(
            states, weights.astype(BF16), (((0,), (0,)), ((), ())), preferred_element_type=F32
        )
        byte_out_ref[:, at] = (block.astype(F32) + mixed / total).astype(BF16)
        return carry

    lax.fori_loop(0, n_bytes // size, cross_step, 0)

    qkv_copy.wait_send()
    for g in (in_gather, down_gather, kv_gather, ps_gather, pool_x, emb_x, att_x):
        g.drain()
    for d in range(1, n_z):
        source = lax.rem(z + n_z - d, n_z)

        @pl.when(core == d % 2)
        def settle(source=source, d=d):
            share(source, d).wait_send()
            pltpu.make_async_remote_copy(
                src_ref=a_src.at[source],
                dst_ref=a_buf.at[source],
                send_sem=zs.at[0, d],
                recv_sem=zr.at[0, source],
                device_id={"seq": source * 2 + y},
                device_id_type=MESH,
            ).wait_send()

    for x in (wo_x, down_x, prj_x):
        x.drain()
    for d in range(1, n_seq):
        rs_copy(d).wait_send()


def body(byte_states, patch_ids, slot_patch, pool_gain, w_in, attn_gain, w_qkv, w_out, w_down):
    n_seq, n_head = lax.axis_size("seq"), lax.axis_size("head")
    rows = slot_patch.shape[0] // n_seq
    n_bytes, cross = byte_states.shape
    width = w_in.shape[1]
    qkv = w_qkv.transpose(1, 0, 2)
    third = w_qkv.shape[2]
    down = w_down.T
    n_z = n_seq // 2
    gains = jnp.pad(
        pool_gain.reshape(n_head, cross), ((0, 0), (0, lanes(cross) - cross))
    ).reshape(-1)
    small = jnp.concatenate([patch_ids.astype(F32), slot_patch.astype(F32), gains])
    small = jnp.pad(small, (0, -small.shape[0] % 1024)).reshape(1, -1)
    vmem = pl.BlockSpec(memory_space=pltpu.VMEM)
    anywhere = pl.BlockSpec(memory_space=pl.ANY)
    dma = pltpu.SemaphoreType.DMA
    n_x = n_head // 2
    stream, byte_out = pl.pallas_call(
        functools.partial(kernel, n_seq, n_head),
        out_shape=(
            jax.ShapeDtypeStruct((rows, width), BF16),
            jax.ShapeDtypeStruct((cross, n_bytes), BF16),
        ),
        in_specs=[vmem] * 3 + [anywhere] * 4,
        out_specs=(vmem, vmem),
        scratch_shapes=[
            pltpu.VMEM((n_seq,) + w_in.shape, BF16),
            pltpu.VMEM((2,) + qkv.shape, BF16),
            pltpu.VMEM((n_seq,) + down.shape, BF16),
            pltpu.VMEM((n_seq, rows, 2 * third), BF16),
            pltpu.VMEM((n_seq, rows, cross), BF16),
            pltpu.VMEM((n_head, w_out.shape[0], width), BF16),
            pltpu.VMEM((n_seq, rows, cross), BF16),
            pltpu.VMEM((n_seq, rows, cross), BF16),
            pltpu.VMEM((n_head, rows, cross), BF16),
            pltpu.VMEM((n_head, rows, width), BF16),
            pltpu.VMEM((n_head, rows, third), BF16),
            pltpu.VMEM((rows, 2 * third), BF16),
            pltpu.VMEM((rows, cross), BF16),
            pltpu.VMEM((n_head, rows, cross), BF16),
            pltpu.VMEM((n_head, rows, cross), BF16),
            pltpu.VMEM((n_seq, rows, 1), F32),
            pltpu.VMEM((rows, cross), BF16),
            pltpu.VMEM((rows, width), BF16),
            pltpu.VMEM((rows, third), BF16),
            pltpu.VMEM((n_z, rows, width), BF16),
            pltpu.VMEM((n_z, rows, width), BF16),
            pltpu.VMEM((n_z, rows, 3 * third), BF16),
            pltpu.VMEM((n_z, rows, 3 * third), BF16),
            dma((4, n_z)),
            dma((4, n_z)),
            dma((4, n_seq)),
            dma((4, 1)),
            dma((3, n_x)),
            dma((3, n_x)),
            dma((3, n_head)),
            dma((3, 1)),
            dma((2, n_head)),
            dma((2, n_head)),
            dma((2, n_z)),
            dma((2, n_z)),
            dma((n_seq,)),
            dma((n_seq,)),
            dma((1,)),
            dma((3,)),
            dma((n_z,)),
        ],
        compiler_params=pltpu.CompilerParams(
            collective_id=0, has_side_effects=True, vmem_limit_bytes=56 * 1024 * 1024
        ),
    )(
        byte_states.T,
        small,
        attn_gain.reshape(n_head, 1, width),
        w_in,
        qkv,
        w_out,
        down,
    )
    return stream, byte_out.T


def solution(mesh):
    placed = (
        P("seq", "head"),
        P("seq"),
        P(),
        P(),
        P("seq", "head"),
        P(),
        P("seq", None, "head"),
        P("head", None),
        P("head", "seq"),
    )
    return jax.shard_map(
        body,
        mesh=mesh,
        in_specs=placed,
        out_specs=(P("seq", "head"), P("seq", "head")),
        check_vma=False,
    )
```
